256 devices in a mesh: rep: 32 (over x_lo, z, core), fsdp: 8 (over x_hi, y).
Axes of the slice: x: 4 (x_hi: 2, x_lo: 2; x = x_hi * 2 + x_lo), y: 4, z: 8, core: 2. Of those that a mesh axis runs over, the one named last changes fastest.
Arguments:
- global_params: bfloat16 [8192, 1024], P('fsdp'), may hold values from -0.0625 to 0.0625
- first_moment: bfloat16 [32, 8192, 1024], P('rep', 'fsdp'), may hold values from -0.19921875 to 0.19921875
- second_moment: bfloat16 [32, 8192, 1024], P('rep', 'fsdp'), may hold values from 9.9658966e-05 to 0.0039978027
- batch: bfloat16 [32, 2, 1024, 8192], P('rep', None, 'fsdp'), may hold values from -6 to 6
- labels: int32 [32, 2, 1024], P('rep', None, 'fsdp'), may hold values from 0 to 1023
- momentum: float32 [8192, 1024], P(('fsdp', 'rep')), may hold values from -0.3 to 0.3
- left_root: bfloat16 [8192, 1024], P(('fsdp', 'rep')), may hold values from -4 to 3
- right_root: bfloat16 [8, 1024, 1024], P('fsdp', 'rep'), may hold values from -4 to 3
Outputs:
- new_params: bfloat16 [8192, 1024], P('fsdp')
- new_momentum: float32 [8192, 1024], P(('fsdp', 'rep'))
The draws below stay inside these ranges and needn't reach their ends.
All inputs are finite; a program needn't handle non-finite values.
Results may differ from the reference program's by a relative error of at most 0.0075.
Values may be sent and summed in bfloat16 or wider, within the bound.
No kernel may reach another device: no remote copies, remote signals or barrier semaphores. Data moves between devices by JAX's collectives and lax.ppermute only.
A program may use at most 128 MiB of HBM per device.

```python
import math
import jax
import jax.numpy as jnp
from jax import lax

D = 8192
KVW = 1024
BLOCK = 1024
TOK_DEV = 128
INNER = 2
TOKENS_R = 1024
REPLICAS = 32
N_REP = 32
N_FSDP = 8


def dominant_rows(key, count, width):
    first_key, second_key = jax.random.split(key)
    rows = jnp.arange(count, dtype=jnp.int32)[:, None]
    columns = jnp.arange(width, dtype=jnp.int32)[None, :]
    diagonal = jax.random.uniform(first_key, (count, 1), jnp.float32, 1.5, 3.0)
    spread = jnp.clip(jax.random.normal(second_key, (count, width), jnp.float32), -4.0, 4.0) / jnp.sqrt(jnp.float32(width))
    return jnp.where(rows % width == columns, diagonal, spread)


def draw_left_root(key, part):
    key = jax.random.fold_in(key, 11)
    return dominant_rows(key, D, BLOCK).astype(jnp.bfloat16)


def draw_right_root(key, part):
    key = jax.random.fold_in(key, 23)
    stacked = dominant_rows(key, D // BLOCK * KVW, KVW)
    return stacked.reshape(D // BLOCK, KVW, KVW).astype(jnp.bfloat16)


def with_ends(values, own_key, smallest, high):
    longest = values.shape.index(max(values.shape))
    spots = []
    for shift in (0, 1):
        where = [jax.random.randint(jax.random.fold_in(own_key, axis), (), 0, length) for axis, length in enumerate(values.shape)]
        where[longest] = (where[longest] + shift) % values.shape[longest]
        spots.append(tuple(where))
    return values.at[spots[0]].set(smallest).at[spots[1]].set(high)


def block_scale(rng, shape, shards, low, high):
    def one(position, blocks):
        steps = jax.random.uniform(jax.random.fold_in(jax.random.fold_in(rng, 6), position), (blocks,), jnp.float32, low / len(shards), high / len(shards))
        return jnp.repeat(jnp.exp(steps), shape[position] // blocks).reshape((-1,) + (1,) * (len(shape) - position - 1))

    factor_of = one(*shards[0])
    for cut in shards[1:]:
        factor_of = factor_of * one(*cut)
    return factor_of


def normal_values(rng, extent, scale, reach, cuts=(), held_as=jnp.bfloat16):
    array = scale * jax.random.normal(rng, extent, jnp.float32)
    if cuts:
        array = array * block_scale(rng, extent, cuts, -0.22, 0.18)
    return jnp.clip(array, -reach, reach).astype(held_as)


def setup_inputs(seed: int = 0) -> dict:
    keys = jax.random.split(jax.random.key(seed), 9)
    return {
        "global_params": normal_values(keys[0], (D, KVW), D ** -0.5, 0.0625, ((0, 8),)),
        "first_moment": normal_values(keys[1], (REPLICAS, D, KVW), 0.03, 0.19921875, ((0, 32), (1, 8))),
        "second_moment": jnp.clip(jnp.exp(math.log(0.0039978027) - 3.6917462 * jax.random.uniform(keys[2], (REPLICAS, D, KVW), jnp.float32) ** block_scale(keys[2], (REPLICAS, D, KVW), ((0, 32), (1, 8)), -0.2, 0.2)), 9.965896606445312e-05, 0.0039978027).astype(jnp.bfloat16),
        "batch": normal_values(keys[3], (REPLICAS, INNER, TOKENS_R, D), 1.0, 6.0, ((0, 32), (2, 8))),
        "labels": with_ends(jax.random.randint(keys[4], (REPLICAS, INNER, TOKENS_R), 0, KVW), jax.random.fold_in(keys[4], 1), 0, KVW - 1).astype(jnp.int32),
        "momentum": normal_values(keys[5], (D, KVW), 0.05, 0.3, ((0, 256),), jnp.float32),
        "left_root": draw_left_root(jax.random.fold_in(keys[8], 71), 0),
        "right_root": draw_right_root(jax.random.fold_in(keys[8], 71), 0),
    }


inner_rate = 0.01
beta_one = 0.9
beta_two = 0.95
adam_eps = 1e-08
decay_rate = 0.1
outer_rate = 0.7
outer_mom = 0.9

def replica_change(params, first, second, inputs, targets):
    weights = params.astype(jnp.float32)
    moment_one = first.astype(jnp.float32)
    moment_two = second.astype(jnp.float32)
    columns = jnp.arange(KVW, dtype=jnp.int32)
    total_tokens = TOK_DEV * N_FSDP
    for step in range(INNER):
        rounded = weights.astype(jnp.bfloat16)
        features = inputs[step]
        projected = jnp.dot(features, rounded, preferred_element_type=jnp.float32)
        target = (targets[step][:, None] == columns[None, :]).astype(jnp.float32)
        residual_grad = ((projected - target) / total_tokens).astype(jnp.bfloat16)
        grad = jnp.zeros((D, KVW), jnp.float32)
        for group in range(N_FSDP):
            rows_in = features[group * TOK_DEV:(group + 1) * TOK_DEV]
            rows_grad = residual_grad[group * TOK_DEV:(group + 1) * TOK_DEV]
            partial_term = lax.dot_general(rows_in, rows_grad, (((0,), (0,)), ((), ())), preferred_element_type=jnp.float32)
            partial_term = lax.optimization_barrier(partial_term.astype(jnp.bfloat16))
            grad = grad + partial_term.astype(jnp.float32)
        count = step + 1
        moment_one = beta_one * moment_one + (1.0 - beta_one) * grad
        moment_two = beta_two * moment_two + (1.0 - beta_two) * grad * grad
        corrected_one = moment_one / (1.0 - beta_one ** count)
        corrected_two = moment_two / (1.0 - beta_two ** count)
        weights = weights - inner_rate * (corrected_one / (jnp.sqrt(corrected_two) + adam_eps) + decay_rate * weights)
    return params.astype(jnp.float32) - weights

def reference(global_params, first_moment, second_moment, batch, labels, momentum, left_root, right_root):

    def accumulate(carry, pieces):
        first, second, inputs, targets = pieces
        return (carry + replica_change(global_params, first, second, inputs, targets), None)
    start = jnp.zeros((D, KVW), jnp.float32)
    delta_sum, _ = lax.scan(accumulate, start, (first_moment, second_moment, batch, labels))
    averaged = delta_sum / N_REP
    blocks = averaged.reshape(D // BLOCK, BLOCK, KVW)
    right_part = jnp.einsum('bik,bkj->bij', blocks, right_root.astype(jnp.float32), precision=lax.Precision.HIGHEST)
    left_blocks = left_root.reshape(D // BLOCK, BLOCK, BLOCK)
    precond = jnp.einsum('bij,bjk->bik', left_blocks.astype(jnp.float32), right_part, precision=lax.Precision.HIGHEST).reshape(D, KVW)
    new_momentum = outer_mom * momentum + precond
    new_params = (global_params.astype(jnp.float32) - outer_rate * (precond + outer_mom * new_momentum)).astype(jnp.bfloat16)
    return (new_params, new_momentum)
```

```python
import jax
import jax.numpy as jnp
from jax import lax
from jax.sharding import PartitionSpec as P

INNER = 2
CHUNKS = 2

inner_rate = 0.01
beta_one = 0.9
beta_two = 0.95
adam_eps = 1e-08
decay_rate = 0.1
outer_rate = 0.7
outer_mom = 0.9


def exchange(pieces, axis, groups=None):
    return lax.all_to_all(pieces, axis, 0, 0, tiled=True, axis_index_groups=groups)


def spread(piece, axis, count, groups=None):
    return exchange(jnp.broadcast_to(piece[None], (count,) + piece.shape), axis, groups)


def shards(
    global_params, first_moment, second_moment, batch, labels, momentum, left_root, right_root
):
    rows, width = global_params.shape
    tokens = batch.shape[2]
    fsdp = lax.axis_size("fsdp")
    replicas = lax.axis_size("rep")
    owned = rows // replicas
    total_tokens = tokens * fsdp
    cols = width // CHUNKS
    own_index = lax.axis_index("rep")
    core = own_index % 2
    swap = [(i, i ^ 1) for i in range(replicas)]
    chips = replicas // 2
    same_core = [[2 * k + c for k in range(chips)] for c in range(2)]

    features = []
    for step in range(INNER):
        split = batch[0, step].reshape(tokens, fsdp, rows).transpose(1, 0, 2)
        features.append(exchange(split, "fsdp").reshape(total_tokens, rows))

    outer = jnp.stack([left_root, right_root[0], momentum.astype(jnp.bfloat16)])
    outer_full = lax.all_gather(outer, "rep", axis=1, tiled=True)
    left_full, right_full, momentum_full = outer_full[0], outer_full[1], outer_full[2]

    start_weights = global_params.astype(jnp.float32)
    state = []
    for chunk in range(CHUNKS):
        part = slice(chunk * cols, (chunk + 1) * cols)
        state.append(
            (
                start_weights[:, part],
                first_moment[0][:, part].astype(jnp.float32),
                second_moment[0][:, part].astype(jnp.float32),
            )
        )
    for step in range(INNER):
        count = step + 1
        for chunk in range(CHUNKS):
            weights, moment_one, moment_two = state[chunk]
            partial = jnp.dot(
                features[step], weights.astype(jnp.bfloat16), preferred_element_type=jnp.float32
            ).astype(jnp.bfloat16)
            arrived = exchange(partial.reshape(fsdp, tokens, cols), "fsdp")
            projected = jnp.sum(arrived.astype(jnp.float32), axis=0)
            columns = jnp.arange(cols, dtype=jnp.int32) + chunk * cols
            target = (labels[0, step][:, None] == columns[None, :]).astype(jnp.float32)
            residual = ((projected - target) / total_tokens).astype(jnp.bfloat16)
            residual = spread(residual, "fsdp", fsdp).reshape(total_tokens, cols)
            grad = lax.dot_general(
                features[step], residual, (((0,), (0,)), ((), ())), preferred_element_type=jnp.float32
            )
            moment_one = beta_one * moment_one + (1.0 - beta_one) * grad
            moment_two = beta_two * moment_two + (1.0 - beta_two) * grad * grad
            corrected_one = moment_one / (1.0 - beta_one**count)
            corrected_two = moment_two / (1.0 - beta_two**count)
            weights = weights - inner_rate * (
                corrected_one / (jnp.sqrt(corrected_two) + adam_eps) + decay_rate * weights
            )
            state[chunk] = (weights, moment_one, moment_two)
    precond = jnp.zeros((rows, width), jnp.float32)
    half = rows // 2
    for chunk in range(CHUNKS):
        part = slice(chunk * cols, (chunk + 1) * cols)
        change = (start_weights[:, part] - state[chunk][0]).reshape(2, half, cols)
        other = lax.dynamic_index_in_dim(change, 1 - core, 0, keepdims=False).astype(jnp.bfloat16)
        mine = lax.dynamic_index_in_dim(change, core, 0, keepdims=False)
        pair = (mine + lax.ppermute(other, "rep", swap).astype(jnp.float32)).astype(jnp.bfloat16)
        arrived = exchange(pair.reshape(chips, half // chips, cols), "rep", same_core)
        total = jnp.sum(arrived.astype(jnp.float32), axis=0)
        averaged = (total / replicas).astype(jnp.bfloat16)
        mine = spread(averaged, "rep", chips, same_core).reshape(half, cols)
        other = lax.ppermute(mine, "rep", swap)
        full = jnp.concatenate(
            [jnp.where(core == 0, mine, other), jnp.where(core == 0, other, mine)], axis=0
        )
        left_part = jnp.dot(left_full, full, preferred_element_type=jnp.float32)
        high = left_part.astype(jnp.bfloat16)
        low = (left_part - high.astype(jnp.float32)).astype(jnp.bfloat16)
        right_rows = right_full[part]
        precond = (
            precond
            + jnp.dot(high, right_rows, preferred_element_type=jnp.float32)
            + jnp.dot(low, right_rows, preferred_element_type=jnp.float32)
        )
    new_params = (
        start_weights
        - outer_rate
        * (
            precond
            + outer_mom * (outer_mom * momentum_full.astype(jnp.float32) + precond)
        )
    ).astype(jnp.bfloat16)
    own = lax.dynamic_slice_in_dim(precond, own_index * owned, owned, 0)
    new_momentum = outer_mom * momentum + own
    return (new_params, new_momentum)


def solution(mesh):
    in_specs = (
        P("fsdp", None),
        P("rep", "fsdp", None),
        P("rep", "fsdp", None),
        P("rep", None, "fsdp", None),
        P("rep", None, "fsdp"),
        P(("fsdp", "rep"), None),
        P(("fsdp", "rep"), None),
        P("fsdp", "rep", None),
    )
    out_specs = (P("fsdp", None), P(("fsdp", "rep"), None))
    return jax.shard_map(shards, mesh=mesh, in_specs=in_specs, out_specs=out_specs, check_vma=False)
```

```python
import functools

import jax
import jax.numpy as jnp
from jax import lax
from jax.experimental import pallas as pl
from jax.experimental.pallas import tpu as pltpu
from jax.sharding import PartitionSpec as P

INNER = 2
BLOCK = 256
SCOPED = 28 * 1024 * 1024

inner_rate = 0.01
beta_one = 0.9
beta_two = 0.95
adam_eps = 1e-08
decay_rate = 0.1
outer_rate = 0.7
outer_mom = 0.9

f32 = jnp.float32
bf16 = jnp.bfloat16
ANY = pl.BlockSpec(memory_space=pl.ANY)


def params():
    return pltpu.CompilerParams(vmem_limit_bytes=SCOPED)


def cost(flops, size):
    return pl.CostEstimate(flops=flops, bytes_accessed=size, transcendentals=0)


def exchange(pieces, axis, groups=None):
    return lax.all_to_all(pieces, axis, 0, 0, tiled=True, axis_index_groups=groups)


def split_kernel(x_ref, o_ref):
    width = o_ref.shape[2]
    for piece in range(o_ref.shape[0]):
        o_ref[piece] = x_ref[0, 0, :, piece * width : (piece + 1) * width]


def split_batch(batch, step, pieces):
    tokens, total = batch.shape[2:]
    width = total // pieces
    per = pieces // 2
    return pl.pallas_call(
        split_kernel,
        grid=(2,),
        in_specs=[pl.BlockSpec((1, 1, tokens, per * width), lambda i: (0, step, 0, i))],
        out_specs=pl.BlockSpec((per, tokens, width), lambda i: (i, 0, 0)),
        out_shape=jax.ShapeDtypeStruct((pieces, tokens, width), batch.dtype),
        compiler_params=params(),
        cost_estimate=cost(0, 4 * tokens * total),
    )(batch)


def hold_kernel(x_ref, *refs):
    pass


def hold(x, *after):
    return pl.pallas_call(
        hold_kernel,
        in_specs=[ANY] * (1 + len(after)),
        out_specs=ANY,
        out_shape=jax.ShapeDtypeStruct(x.shape, x.dtype),
        input_output_aliases={0: 0},
        compiler_params=params(),
    )(x, *after)


def pack_kernel(place_ref, *refs):
    for side in range(2):
        out = refs[7 + side]
        for what in range(3):
            out[what] = refs[3 * side + what][...].reshape(out.shape[1:]).astype(bf16)


def pack(place, left, right, momentum, after):
    owned, width = left.shape
    half = width // 2

    def specs(side):
        def column(p):
            return lax.rem(p[0] + side, 2)

        return [
            pl.BlockSpec((owned, half), lambda i, p: (0, column(p))),
            pl.BlockSpec((1, owned, half), lambda i, p: (0, 0, column(p))),
            pl.BlockSpec((owned, half), lambda i, p: (0, column(p))),
        ]

    return pl.pallas_call(
        pack_kernel,
        grid_spec=pltpu.PrefetchScalarGridSpec(
            num_scalar_prefetch=1,
            grid=(1,),
            in_specs=specs(0) + specs(1) + [ANY],
            out_specs=[pl.BlockSpec((3, owned, half), lambda i, p: (0, 0, 0))] * 2,
        ),
        out_shape=[jax.ShapeDtypeStruct((3, owned, half), bf16)] * 2,
        compiler_params=params(),
        cost_estimate=cost(0, 16 * owned * width),
    )(place, *([left, right, momentum] * 2), after)


def flat(ref):
    return ref[...].reshape(-1, ref.shape[-1])


def partial_kernel(x_ref, w_ref, after_ref, o_ref):
    term = jnp.dot(flat(x_ref), w_ref[...], preferred_element_type=f32)
    o_ref[...] = term.astype(bf16).reshape(o_ref.shape)


def partial_of(features, weights, after):
    pieces, tokens, rows = features.shape
    width = weights.shape[1]
    per = pieces // 2
    return pl.pallas_call(
        partial_kernel,
        grid=(2,),
        in_specs=[
            pl.BlockSpec((per, tokens, rows), lambda i: (i, 0, 0)),
            pl.BlockSpec((rows, width), lambda i: (0, 0)),
            ANY,
        ],
        out_specs=pl.BlockSpec((per, tokens, width), lambda i: (i, 0, 0)),
        out_shape=jax.ShapeDtypeStruct((pieces, tokens, width), bf16),
        compiler_params=params(),
        cost_estimate=cost(2 * pieces * tokens * rows * width, 6 * rows * width),
    )(features, weights, after)


def residual_kernel(total_tokens, a_ref, l_ref, o_ref):
    count, tokens, cols = a_ref.shape
    projected = a_ref[0].astype(f32)
    for piece in range(1, count):
        projected = projected + a_ref[piece].astype(f32)
    columns = lax.broadcasted_iota(jnp.int32, (tokens, cols), 1) + pl.program_id(0) * cols
    target = jnp.where(l_ref[...] == columns, 1.0, 0.0)
    residual = ((projected - target) / total_tokens).astype(bf16)
    for piece in range(count):
        o_ref[piece] = residual


def spread_residual(arrived, labels, total_tokens):
    count, tokens, width = arrived.shape
    spec = pl.BlockSpec((count, tokens, width // 2), lambda i: (0, 0, i))
    return pl.pallas_call(
        functools.partial(residual_kernel, total_tokens),
        grid=(2,),
        in_specs=[spec, pl.BlockSpec((tokens, 1), lambda i: (0, 0))],
        out_specs=spec,
        out_shape=jax.ShapeDtypeStruct(arrived.shape, bf16),
        compiler_params=params(),
        cost_estimate=cost(0, 4 * arrived.size),
    )(arrived, labels)


def average_kernel(scale, a_ref, o_ref):
    total = a_ref[0].astype(f32)
    for piece in range(1, a_ref.shape[0]):
        total = total + a_ref[piece].astype(f32)
    averaged = (total / scale).astype(bf16)
    for piece in range(a_ref.shape[0]):
        o_ref[piece] = averaged


def spread_average(arrived, scale):
    return pl.pallas_call(
        functools.partial(average_kernel, scale),
        out_shape=jax.ShapeDtypeStruct(arrived.shape, bf16),
        compiler_params=params(),
        cost_estimate=cost(0, 4 * arrived.size),
    )(arrived)


def adam(count, grad, weights, moment_one, moment_two):
    moment_one = beta_one * moment_one + (1.0 - beta_one) * grad
    moment_two = beta_two * moment_two + ((1.0 - beta_two) * grad) * grad
    corrected = moment_two * (1.0 / (1.0 - beta_two**count))
    root = corrected * lax.rsqrt(corrected)
    scaled = (inner_rate / (1.0 - beta_one**count)) * moment_one
    weights = (1.0 - inner_rate * decay_rate) * weights - scaled * pltpu.reciprocal(root + adam_eps)
    return weights, moment_one, moment_two


def turned_dot(x, r):
    return lax.dot_general(x, r, (((0,), (0,)), ((), ())), preferred_element_type=f32)


def middle_kernel(x_ref, r_ref, w_ref, m_ref, v_ref, wo_ref, mo_ref, vo_ref, rounded_ref):
    weights, moment_one, moment_two = adam(
        1,
        turned_dot(flat(x_ref), flat(r_ref)),
        w_ref[...].astype(f32),
        m_ref[0].astype(f32),
        v_ref[0].astype(f32),
    )
    wo_ref[...] = weights
    mo_ref[...] = moment_one
    vo_ref[...] = moment_two
    rounded_ref[...] = weights.astype(bf16)


def middle(features, residual, weights, first, second):
    pieces, tokens, rows = features.shape
    width = weights.shape[1]
    block = BLOCK
    state = jax.ShapeDtypeStruct((rows, width), f32)
    state_spec = pl.BlockSpec((block, width), lambda i: (i, 0))
    moment_spec = pl.BlockSpec((1, block, width), lambda i: (0, i, 0))
    return pl.pallas_call(
        middle_kernel,
        grid=(rows // block,),
        in_specs=[
            pl.BlockSpec((pieces, tokens, block), lambda i: (0, 0, i)),
            pl.BlockSpec((pieces, tokens, width), lambda i: (0, 0, 0)),
            state_spec,
            moment_spec,
            moment_spec,
        ],
        out_specs=[state_spec] * 4,
        out_shape=[state] * 3 + [jax.ShapeDtypeStruct((rows, width), bf16)],
        compiler_params=params(),
        cost_estimate=cost(2 * pieces * tokens * rows * width, 26 * rows * width),
    )(features, residual, weights, first, second)


def last_kernel(place_ref, x_ref, r_ref, g_ref, w_ref, m_ref, v_ref, mine_ref, other_ref):
    grad = turned_dot(flat(x_ref), flat(r_ref))
    weights, _, _ = adam(INNER, grad, w_ref[...], m_ref[...], v_ref[...])
    change = g_ref[...].astype(f32) - weights
    step, half = pl.program_id(0), pl.num_programs(0) // 2

    @pl.when(step < half)
    def _():
        other_ref[...] = change.astype(bf16)

    @pl.when(step >= half)
    def _():
        mine_ref[...] = change


def last(place, features, residual, start, state):
    pieces, tokens, rows = features.shape
    width = start.shape[1]
    block = BLOCK
    steps = rows // block
    half = steps // 2

    def row(i, p):
        return lax.rem(i + half * (1 + p[0]), steps)

    state_spec = pl.BlockSpec((block, width), lambda i, p: (row(i, p), 0))
    return pl.pallas_call(
        last_kernel,
        grid_spec=pltpu.PrefetchScalarGridSpec(
            num_scalar_prefetch=1,
            grid=(steps,),
            in_specs=[
                pl.BlockSpec((pieces, tokens, block), lambda i, p: (0, 0, row(i, p))),
                pl.BlockSpec((pieces, tokens, width), lambda i, p: (0, 0, 0)),
            ]
            + [state_spec] * 4,
            out_specs=[
                pl.BlockSpec((block, width), lambda i, p: (jnp.maximum(i - half, 0), 0)),
                pl.BlockSpec((block, width), lambda i, p: (jnp.minimum(i, half - 1), 0)),
            ],
        ),
        out_shape=[
            jax.ShapeDtypeStruct((rows // 2, width), f32),
            jax.ShapeDtypeStruct((rows // 2, width), bf16),
        ],
        compiler_params=params(),
        cost_estimate=cost(2 * pieces * tokens * rows * width, 20 * rows * width),
    )(place, features, residual, start, *state)


def outer_kernel(
    place_ref, near_left, far_left, near_low, near_high, far_low, far_high, near_mom, far_mom,
    mine_ref, other_ref, g_ref, own_ref, new_ref, new_mom_ref, left, kept,
):
    side, row = pl.program_id(0), pl.program_id(1)
    half, width = mine_ref.shape

    def square(ref):
        return ref[...].reshape(half, half)

    @pl.when(side == 0)
    def _():
        left_part = jnp.dot(square(near_left), mine_ref[...], preferred_element_type=f32) + jnp.dot(
            square(far_left), other_ref[...], preferred_element_type=f32
        )
        left[row] = left_part.astype(bf16)

    def finish(first, second, mom_ref):
        precond = jnp.dot(left[row, :, :half], square(first), preferred_element_type=f32) + jnp.dot(
            left[row, :, half:], square(second), preferred_element_type=f32
        )
        momentum = outer_mom * square(mom_ref).astype(f32) + precond
        new_ref[...] = (
            g_ref[...].astype(f32) - outer_rate * (precond + outer_mom * momentum)
        ).astype(bf16)
        owned = own_ref.shape[0]
        per = half // owned

        @pl.when(row == place_ref[1] // per)
        def _():
            kept[...] = precond
            start = pl.multiple_of(lax.rem(place_ref[1], per) * owned, owned)
            new_mom_ref[...] = outer_mom * own_ref[...] + kept[pl.ds(start, owned), :]

    @pl.when(side == 0)
    def _():
        finish(near_low, near_high, near_mom)

    @pl.when(side == 1)
    def _():
        finish(far_low, far_high, far_mom)


def outer(place, near, far, mine, other, start, momentum):
    depth, _, cores, _, owned, half = near.shape
    width = mine.shape[1]

    def piece(what, row):
        return pl.BlockSpec(
            (depth, 1, cores, 1, owned, half), lambda j, i, p: (0, row(i), 0, what, 0, 0)
        )

    def here(i):
        return i

    def column(j, p):
        return lax.rem(p[0] + j, 2)

    low, high = (lambda i: 0), (lambda i: 1)
    whole = pl.BlockSpec((half, width), lambda j, i, p: (0, 0))
    own_spec = pl.BlockSpec((owned, half), lambda j, i, p: (0, column(j, p)))
    new_spec = pl.BlockSpec((half, half), lambda j, i, p: (i, column(j, p)))
    return pl.pallas_call(
        outer_kernel,
        grid_spec=pltpu.PrefetchScalarGridSpec(
            num_scalar_prefetch=1,
            grid=(2, 2),
            in_specs=[
                piece(0, here),
                piece(0, here),
                piece(1, low),
                piece(1, high),
                piece(1, low),
                piece(1, high),
                piece(2, here),
                piece(2, here),
                whole,
                whole,
                new_spec,
                own_spec,
            ],
            out_specs=[new_spec, own_spec],
            scratch_shapes=[
                pltpu.VMEM((2, half, width), bf16),
                pltpu.VMEM((half, half), f32),
            ],
        ),
        out_shape=[
            jax.ShapeDtypeStruct((2 * half, width), bf16),
            jax.ShapeDtypeStruct((owned, width), f32),
        ],
        compiler_params=params(),
        cost_estimate=cost(4 * width**3, 14 * width * width),
    )(place, near, far, near, near, far, far, near, far, mine, other, start, momentum)


def shards(
    global_params, first_moment, second_moment, batch, labels, momentum, left_root, right_root
):
    rows, width = global_params.shape
    tokens = batch.shape[2]
    fsdp = lax.axis_size("fsdp")
    replicas = lax.axis_size("rep")
    owned = rows // replicas
    total_tokens = tokens * fsdp
    half = rows // 2
    own_index = lax.axis_index("rep")
    core = own_index % 2
    upper = own_index // (replicas // 2)

    def stamp(kind):
        return jnp.stack([core, own_index, own_index * 4 + kind]).astype(jnp.int32)

    chips = replicas // 2
    depth = chips // 2
    swap = [(i, i ^ 1) for i in range(replicas)]
    beside = [(i, i ^ chips) for i in range(replicas)]
    same_core = [[2 * k + c for k in range(chips)] for c in range(2)]
    column = [[x * chips + 2 * z + c for z in range(depth)] for x in range(2) for c in range(2)]
    targets = [labels[0, step].reshape(tokens, 1) for step in range(INNER)]

    features = exchange(split_batch(batch, 0, fsdp), "fsdp")
    split = split_batch(batch, 1, fsdp)
    partial = partial_of(features, global_params, split)

    def ordered(index, own, partner):
        return jnp.where(index == 0, jnp.stack([own, partner]), jnp.stack([partner, own]))

    def own_residual(partial, step):
        return spread_residual(exchange(partial, "fsdp"), targets[step], total_tokens)

    own = own_residual(partial, 0)
    residual = exchange(own, "fsdp")
    kept, sent = pack(stamp(1), left_root, right_root, momentum, own)
    two = ordered(core, kept, lax.ppermute(sent, "rep", swap))
    four = ordered(upper, two, lax.ppermute(two, "rep", beside))
    near = lax.all_gather(four, "rep", axis=0, axis_index_groups=column)
    far = lax.ppermute(near, "rep", swap)
    following = exchange(hold(split, residual, four), "fsdp")
    *state, rounded = middle(features, residual, global_params, first_moment, second_moment)
    partial = partial_of(following, rounded, rounded)
    mine, sent = last(stamp(3), following, exchange(own_residual(partial, 1), "fsdp"), global_params, state)
    pair = (mine + lax.ppermute(sent, "rep", swap).astype(f32)).astype(bf16)
    arrived = exchange(pair.reshape(chips, owned, width), "rep", same_core)
    averaged = exchange(spread_average(arrived, replicas), "rep", same_core).reshape(half, width)
    other = lax.ppermute(averaged, "rep", swap)
    return tuple(outer(stamp(5), near, far, averaged, other, global_params, momentum))


def solution(mesh):
    in_specs = (
        P("fsdp", None),
        P("rep", "fsdp", None),
        P("rep", "fsdp", None),
        P("rep", None, "fsdp", None),
        P("rep", None, "fsdp"),
        P(("fsdp", "rep"), None),
        P(("fsdp", "rep"), None),
        P("fsdp", "rep", None),
    )
    out_specs = (P("fsdp", None), P(("fsdp", "rep"), None))
    return jax.shard_map(shards, mesh=mesh, in_specs=in_specs, out_specs=out_specs, check_vma=False)
```

```python
import functools

import jax
import jax.numpy as jnp
from jax import lax
from jax.experimental import pallas as pl
from jax.experimental.pallas import tpu as pltpu
from jax.sharding import PartitionSpec as P

INNER = 2
BLOCK = 256
SCOPED = 28 * 1024 * 1024

inner_rate = 0.01
beta_one = 0.9
beta_two = 0.95
adam_eps = 1e-08
decay_rate = 0.1
outer_rate = 0.7
outer_mom = 0.9

f32 = jnp.float32
bf16 = jnp.bfloat16
ANY = pl.BlockSpec(memory_space=pl.ANY)


def params():
    return pltpu.CompilerParams(vmem_limit_bytes=SCOPED)


def cost(flops, size):
    return pl.CostEstimate(flops=flops, bytes_accessed=size, transcendentals=0)


def apart(x):
    return pltpu.with_memory_space_constraint(x, pltpu.HBM)


def exchange(pieces, axis, groups=None):
    return lax.all_to_all(pieces, axis, 0, 0, tiled=True, axis_index_groups=groups)


def split_kernel(x_ref, o_ref):
    width = o_ref.shape[2]
    for piece in range(o_ref.shape[0]):
        o_ref[piece] = x_ref[0, 0, :, piece * width : (piece + 1) * width]


def split_batch(batch, step, pieces):
    tokens, total = batch.shape[2:]
    width = total // pieces
    per = pieces // 2
    return pl.pallas_call(
        split_kernel,
        grid=(2,),
        in_specs=[pl.BlockSpec((1, 1, tokens, per * width), lambda i: (0, step, 0, i))],
        out_specs=pl.BlockSpec((per, tokens, width), lambda i: (i, 0, 0)),
        out_shape=jax.ShapeDtypeStruct((pieces, tokens, width), batch.dtype),
        compiler_params=params(),
        cost_estimate=cost(0, 4 * tokens * total),
    )(apart(batch))


def hold_kernel(x_ref, *refs):
    pass


def hold(x, *after):
    return pl.pallas_call(
        hold_kernel,
        in_specs=[ANY] * (1 + len(after)),
        out_specs=ANY,
        out_shape=jax.ShapeDtypeStruct(x.shape, x.dtype),
        input_output_aliases={0: 0},
        compiler_params=params(),
    )(x, *after)


def pack_kernel(place_ref, *refs):
    for side in range(2):
        out = refs[7 + side]
        for what in range(3):
            out[what] = refs[3 * side + what][...].reshape(out.shape[1:]).astype(bf16)


def pack(place, left, right, momentum, after):
    owned, width = left.shape
    half = width // 2

    def specs(side):
        def column(p):
            return lax.rem(p[0] + side, 2)

        return [
            pl.BlockSpec((owned, half), lambda i, p: (0, column(p))),
            pl.BlockSpec((1, owned, half), lambda i, p: (0, 0, column(p))),
            pl.BlockSpec((owned, half), lambda i, p: (0, column(p))),
        ]

    return pl.pallas_call(
        pack_kernel,
        grid_spec=pltpu.PrefetchScalarGridSpec(
            num_scalar_prefetch=1,
            grid=(1,),
            in_specs=specs(0) + specs(1) + [ANY],
            out_specs=[pl.BlockSpec((3, owned, half), lambda i, p: (0, 0, 0))] * 2,
        ),
        out_shape=[jax.ShapeDtypeStruct((3, owned, half), bf16)] * 2,
        compiler_params=params(),
        cost_estimate=cost(0, 16 * owned * width),
    )(place, *([left, right, momentum] * 2), after)


def flat(ref):
    return ref[...].reshape(-1, ref.shape[-1])


def partial_kernel(x_ref, w_ref, after_ref, o_ref):
    term = jnp.dot(flat(x_ref), w_ref[...], preferred_element_type=f32)
    o_ref[...] = term.astype(bf16).reshape(o_ref.shape)


def partial_of(features, weights, after):
    pieces, tokens, rows = features.shape
    width = weights.shape[1]
    per = pieces // 2
    return pl.pallas_call(
        partial_kernel,
        grid=(2,),
        in_specs=[
            pl.BlockSpec((per, tokens, rows), lambda i: (i, 0, 0)),
            pl.BlockSpec((rows, width), lambda i: (0, 0)),
            ANY,
        ],
        out_specs=pl.BlockSpec((per, tokens, width), lambda i: (i, 0, 0)),
        out_shape=pltpu.HBM((pieces, tokens, width), bf16),
        compiler_params=params(),
        cost_estimate=cost(2 * pieces * tokens * rows * width, 6 * rows * width),
    )(features, weights, after)


def residual_kernel(total_tokens, a_ref, l_ref, o_ref):
    count, tokens, cols = a_ref.shape
    projected = a_ref[0].astype(f32)
    for piece in range(1, count):
        projected = projected + a_ref[piece].astype(f32)
    columns = lax.broadcasted_iota(jnp.int32, (tokens, cols), 1) + pl.program_id(0) * cols
    target = jnp.where(l_ref[...] == columns, 1.0, 0.0)
    residual = ((projected - target) / total_tokens).astype(bf16)
    for piece in range(count):
        o_ref[piece] = residual


def spread_residual(arrived, labels, total_tokens):
    count, tokens, width = arrived.shape
    spec = pl.BlockSpec((count, tokens, width // 2), lambda i: (0, 0, i))
    return pl.pallas_call(
        functools.partial(residual_kernel, total_tokens),
        grid=(2,),
        in_specs=[spec, pl.BlockSpec((tokens, 1), lambda i: (0, 0))],
        out_specs=spec,
        out_shape=pltpu.HBM(arrived.shape, bf16),
        compiler_params=params(),
        cost_estimate=cost(0, 4 * arrived.size),
    )(arrived, labels)


def average_kernel(scale, a_ref, o_ref):
    total = a_ref[0].astype(f32)
    for piece in range(1, a_ref.shape[0]):
        total = total + a_ref[piece].astype(f32)
    averaged = (total / scale).astype(bf16)
    for piece in range(a_ref.shape[0]):
        o_ref[piece] = averaged


def spread_average(arrived, scale):
    return pl.pallas_call(
        functools.partial(average_kernel, scale),
        out_shape=jax.ShapeDtypeStruct(arrived.shape, bf16),
        compiler_params=params(),
        cost_estimate=cost(0, 4 * arrived.size),
    )(arrived)


def adam(count, grad, weights, moment_one, moment_two):
    moment_one = beta_one * moment_one + (1.0 - beta_one) * grad
    moment_two = beta_two * moment_two + ((1.0 - beta_two) * grad) * grad
    corrected = moment_two * (1.0 / (1.0 - beta_two**count))
    root = corrected * lax.rsqrt(corrected)
    scaled = (inner_rate / (1.0 - beta_one**count)) * moment_one
    weights = (1.0 - inner_rate * decay_rate) * weights - scaled * pltpu.reciprocal(root + adam_eps)
    return weights, moment_one, moment_two


def turned_dot(x, r):
    return lax.dot_general(x, r, (((0,), (0,)), ((), ())), preferred_element_type=f32)


def middle_kernel(x_ref, r_ref, w_ref, m_ref, v_ref, wo_ref, mo_ref, vo_ref, rounded_ref):
    weights, moment_one, moment_two = adam(
        1,
        turned_dot(flat(x_ref), flat(r_ref)),
        w_ref[...].astype(f32),
        m_ref[0].astype(f32),
        v_ref[0].astype(f32),
    )
    wo_ref[...] = weights
    mo_ref[...] = moment_one
    vo_ref[...] = moment_two
    rounded_ref[...] = weights.astype(bf16)


def middle(features, residual, weights, first, second):
    pieces, tokens, rows = features.shape
    width = weights.shape[1]
    block = BLOCK
    state = jax.ShapeDtypeStruct((rows, width), f32)
    state_spec = pl.BlockSpec((block, width), lambda i: (i, 0))
    moment_spec = pl.BlockSpec((1, block, width), lambda i: (0, i, 0))
    return pl.pallas_call(
        middle_kernel,
        grid=(rows // block,),
        in_specs=[
            pl.BlockSpec((pieces, tokens, block), lambda i: (0, 0, i)),
            pl.BlockSpec((pieces, tokens, width), lambda i: (0, 0, 0)),
            state_spec,
            moment_spec,
            moment_spec,
        ],
        out_specs=[state_spec] * 4,
        out_shape=[state] * 3 + [jax.ShapeDtypeStruct((rows, width), bf16)],
        compiler_params=params(),
        cost_estimate=cost(2 * pieces * tokens * rows * width, 26 * rows * width),
    )(features, residual, weights, first, second)


def last_kernel(place_ref, x_ref, r_ref, g_ref, w_ref, m_ref, v_ref, mine_ref, other_ref):
    grad = turned_dot(flat(x_ref), flat(r_ref))
    weights, _, _ = adam(INNER, grad, w_ref[...], m_ref[...], v_ref[...])
    change = g_ref[...].astype(f32) - weights
    step, half = pl.program_id(0), pl.num_programs(0) // 2

    @pl.when(step < half)
    def _():
        other_ref[...] = change.astype(bf16)

    @pl.when(step >= half)
    def _():
        mine_ref[...] = change


def last(place, features, residual, start, state):
    pieces, tokens, rows = features.shape
    width = start.shape[1]
    block = BLOCK
    steps = rows // block
    half = steps // 2

    def row(i, p):
        return lax.rem(i + half * (1 + p[0]), steps)

    state_spec = pl.BlockSpec((block, width), lambda i, p: (row(i, p), 0))
    return pl.pallas_call(
        last_kernel,
        grid_spec=pltpu.PrefetchScalarGridSpec(
            num_scalar_prefetch=1,
            grid=(steps,),
            in_specs=[
                pl.BlockSpec((pieces, tokens, block), lambda i, p: (0, 0, row(i, p))),
                pl.BlockSpec((pieces, tokens, width), lambda i, p: (0, 0, 0)),
            ]
            + [state_spec] * 4,
            out_specs=[
                pl.BlockSpec((block, width), lambda i, p: (jnp.maximum(i - half, 0), 0)),
                pl.BlockSpec((block, width), lambda i, p: (jnp.minimum(i, half - 1), 0)),
            ],
        ),
        out_shape=[
            jax.ShapeDtypeStruct((rows // 2, width), f32),
            jax.ShapeDtypeStruct((rows // 2, width), bf16),
        ],
        compiler_params=params(),
        cost_estimate=cost(2 * pieces * tokens * rows * width, 20 * rows * width),
    )(place, features, residual, start, *state)


def outer_kernel(
    place_ref, near_left, far_left, near_low, near_high, far_low, far_high, near_mom, far_mom,
    mine_ref, other_ref, g_ref, own_ref, new_ref, new_mom_ref, left, kept,
):
    side, row = pl.program_id(0), pl.program_id(1)
    half, width = mine_ref.shape

    def square(ref):
        return ref[...].reshape(half, half)

    @pl.when(side == 0)
    def _():
        left_part = jnp.dot(square(near_left), mine_ref[...], preferred_element_type=f32) + jnp.dot(
            square(far_left), other_ref[...], preferred_element_type=f32
        )
        left[row] = left_part.astype(bf16)

    def finish(first, second, mom_ref):
        precond = jnp.dot(left[row, :, :half], square(first), preferred_element_type=f32) + jnp.dot(
            left[row, :, half:], square(second), preferred_element_type=f32
        )
        momentum = outer_mom * square(mom_ref).astype(f32) + precond
        new_ref[...] = (
            g_ref[...].astype(f32) - outer_rate * (precond + outer_mom * momentum)
        ).astype(bf16)
        owned = own_ref.shape[0]
        per = half // owned

        @pl.when(row == place_ref[1] // per)
        def _():
            kept[...] = precond
            start = pl.multiple_of(lax.rem(place_ref[1], per) * owned, owned)
            new_mom_ref[...] = outer_mom * own_ref[...] + kept[pl.ds(start, owned), :]

    @pl.when(side == 0)
    def _():
        finish(near_low, near_high, near_mom)

    @pl.when(side == 1)
    def _():
        finish(far_low, far_high, far_mom)


def outer(place, near, far, mine, other, start, momentum):
    depth, _, cores, _, owned, half = near.shape
    width = mine.shape[1]

    def piece(what, row):
        return pl.BlockSpec(
            (depth, 1, cores, 1, owned, half), lambda j, i, p: (0, row(i), 0, what, 0, 0)
        )

    def here(i):
        return i

    def column(j, p):
        return lax.rem(p[0] + j, 2)

    low, high = (lambda i: 0), (lambda i: 1)
    whole = pl.BlockSpec((half, width), lambda j, i, p: (0, 0))
    own_spec = pl.BlockSpec((owned, half), lambda j, i, p: (0, column(j, p)))
    new_spec = pl.BlockSpec((half, half), lambda j, i, p: (i, column(j, p)))
    return pl.pallas_call(
        outer_kernel,
        grid_spec=pltpu.PrefetchScalarGridSpec(
            num_scalar_prefetch=1,
            grid=(2, 2),
            in_specs=[
                piece(0, here),
                piece(0, here),
                piece(1, low),
                piece(1, high),
                piece(1, low),
                piece(1, high),
                piece(2, here),
                piece(2, here),
                whole,
                whole,
                new_spec,
                own_spec,
            ],
            out_specs=[new_spec, own_spec],
            scratch_shapes=[
                pltpu.VMEM((2, half, width), bf16),
                pltpu.VMEM((half, half), f32),
            ],
        ),
        out_shape=[
            jax.ShapeDtypeStruct((2 * half, width), bf16),
            jax.ShapeDtypeStruct((owned, width), f32),
        ],
        compiler_params=params(),
        cost_estimate=cost(4 * width**3, 14 * width * width),
    )(place, near, far, near, near, far, far, near, far, mine, other, start, momentum)


def shards(
    global_params, first_moment, second_moment, batch, labels, momentum, left_root, right_root
):
    rows, width = global_params.shape
    tokens = batch.shape[2]
    fsdp = lax.axis_size("fsdp")
    replicas = lax.axis_size("rep")
    owned = rows // replicas
    total_tokens = tokens * fsdp
    half = rows // 2
    own_index = lax.axis_index("rep")
    core = own_index % 2
    upper = own_index // (replicas // 2)

    def stamp(kind):
        return jnp.stack([core, own_index, own_index * 4 + kind]).astype(jnp.int32)

    chips = replicas // 2
    depth = chips // 2
    swap = [(i, i ^ 1) for i in range(replicas)]
    beside = [(i, i ^ chips) for i in range(replicas)]
    same_core = [[2 * k + c for k in range(chips)] for c in range(2)]
    column = [[x * chips + 2 * z + c for z in range(depth)] for x in range(2) for c in range(2)]
    targets = [labels[0, step].reshape(tokens, 1) for step in range(INNER)]

    features = exchange(split_batch(batch, 0, fsdp), "fsdp")
    split = split_batch(batch, 1, fsdp)
    partial = partial_of(features, global_params, split)

    def ordered(index, own, partner):
        return jnp.where(index == 0, jnp.stack([own, partner]), jnp.stack([partner, own]))

    def own_residual(partial, step):
        return spread_residual(exchange(partial, "fsdp"), targets[step], total_tokens)

    own = own_residual(partial, 0)
    residual = exchange(own, "fsdp")
    kept, sent = pack(stamp(1), left_root, right_root, momentum, own)
    two = ordered(core, kept, lax.ppermute(sent, "rep", swap))
    four = ordered(upper, two, lax.ppermute(two, "rep", beside))
    near = lax.all_gather(four, "rep", axis=0, axis_index_groups=column)
    far = lax.ppermute(near, "rep", swap)
    following = exchange(hold(split, residual, four), "fsdp")
    *state, rounded = middle(
        features, residual, global_params, apart(first_moment), apart(second_moment)
    )
    state = [apart(x) for x in state]
    partial = partial_of(following, apart(rounded), residual)
    mine, sent = last(stamp(3), following, exchange(own_residual(partial, 1), "fsdp"), global_params, state)
    pair = (mine + lax.ppermute(sent, "rep", swap).astype(f32)).astype(bf16)
    arrived = exchange(pair.reshape(chips, owned, width), "rep", same_core)
    averaged = exchange(spread_average(arrived, replicas), "rep", same_core).reshape(half, width)
    other = lax.ppermute(averaged, "rep", swap)
    return tuple(outer(stamp(5), near, far, averaged, other, global_params, momentum))


def solution(mesh):
    in_specs = (
        P("fsdp", None),
        P("rep", "fsdp", None),
        P("rep", "fsdp", None),
        P("rep", None, "fsdp", None),
        P("rep", None, "fsdp"),
        P(("fsdp", "rep"), None),
        P(("fsdp", "rep"), None),
        P("fsdp", "rep", None),
    )
    out_specs = (P("fsdp", None), P(("fsdp", "rep"), None))
    return jax.shard_map(shards, mesh=mesh, in_specs=in_specs, out_specs=out_specs, check_vma=False)
```

```python
import functools

import jax
import jax.numpy as jnp
from jax import lax
from jax.experimental import pallas as pl
from jax.experimental.pallas import tpu as pltpu
from jax.sharding import PartitionSpec as P

INNER = 2
BLOCK = 256
SCOPED = 22 * 1024 * 1024

inner_rate = 0.01
beta_one = 0.9
beta_two = 0.95
adam_eps = 1e-08
decay_rate = 0.1
outer_rate = 0.7
outer_mom = 0.9

f32 = jnp.float32
bf16 = jnp.bfloat16
ANY = pl.BlockSpec(memory_space=pl.ANY)


def params():
    return pltpu.CompilerParams(vmem_limit_bytes=SCOPED)


def cost(flops, size):
    return pl.CostEstimate(flops=flops, bytes_accessed=size, transcendentals=0)


def apart(x):
    return pltpu.with_memory_space_constraint(x, pltpu.HBM)


def exchange(pieces, axis, groups=None):
    return lax.all_to_all(pieces, axis, 0, 0, tiled=True, axis_index_groups=groups)


def split_kernel(x_ref, o_ref):
    width = o_ref.shape[2]
    for piece in range(o_ref.shape[0]):
        o_ref[piece] = x_ref[0, 0, :, piece * width : (piece + 1) * width]


def split_batch(batch, step, pieces):
    tokens, total = batch.shape[2:]
    width = total // pieces
    per = pieces // 2
    return pl.pallas_call(
        split_kernel,
        grid=(2,),
        in_specs=[pl.BlockSpec((1, 1, tokens, per * width), lambda i: (0, step, 0, i))],
        out_specs=pl.BlockSpec((per, tokens, width), lambda i: (i, 0, 0)),
        out_shape=jax.ShapeDtypeStruct((pieces, tokens, width), batch.dtype),
        compiler_params=params(),
        cost_estimate=cost(0, 4 * tokens * total),
    )(apart(batch))


def hold_kernel(x_ref, *refs):
    pass


def hold(x, *after):
    return pl.pallas_call(
        hold_kernel,
        in_specs=[ANY] * (1 + len(after)),
        out_specs=ANY,
        out_shape=jax.ShapeDtypeStruct(x.shape, x.dtype),
        input_output_aliases={0: 0},
        compiler_params=params(),
    )(x, *after)


def pack_kernel(place_ref, *refs):
    for side in range(2):
        out = refs[7 + side]
        for what in range(3):
            out[what] = refs[3 * side + what][...].reshape(out.shape[1:]).astype(bf16)


def pack(place, left, right, momentum, after):
    owned, width = left.shape
    half = width // 2

    def specs(side):
        def column(p):
            return lax.rem(p[0] + side, 2)

        return [
            pl.BlockSpec((owned, half), lambda i, p: (0, column(p))),
            pl.BlockSpec((1, owned, half), lambda i, p: (0, 0, column(p))),
            pl.BlockSpec((owned, half), lambda i, p: (0, column(p))),
        ]

    return pl.pallas_call(
        pack_kernel,
        grid_spec=pltpu.PrefetchScalarGridSpec(
            num_scalar_prefetch=1,
            grid=(1,),
            in_specs=specs(0) + specs(1) + [ANY],
            out_specs=[pl.BlockSpec((3, owned, half), lambda i, p: (0, 0, 0))] * 2,
        ),
        out_shape=[jax.ShapeDtypeStruct((3, owned, half), bf16)] * 2,
        compiler_params=params(),
        cost_estimate=cost(0, 16 * owned * width),
    )(place, *([left, right, momentum] * 2), after)


def flat(ref):
    return ref[...].reshape(-1, ref.shape[-1])


def partial_kernel(x_ref, w_ref, after_ref, o_ref):
    term = jnp.dot(flat(x_ref), w_ref[...], preferred_element_type=f32)
    o_ref[...] = term.astype(bf16).reshape(o_ref.shape)


def partial_of(features, weights, after):
    pieces, tokens, rows = features.shape
    width = weights.shape[1]
    per = pieces // 2
    return pl.pallas_call(
        partial_kernel,
        grid=(2,),
        in_specs=[
            pl.BlockSpec((per, tokens, rows), lambda i: (i, 0, 0)),
            pl.BlockSpec((rows, width), lambda i: (0, 0)),
            ANY,
        ],
        out_specs=pl.BlockSpec((per, tokens, width), lambda i: (i, 0, 0)),
        out_shape=pltpu.HBM((pieces, tokens, width), bf16),
        compiler_params=params(),
        cost_estimate=cost(2 * pieces * tokens * rows * width, 6 * rows * width),
    )(features, weights, after)


def residual_kernel(total_tokens, a_ref, l_ref, o_ref):
    count, tokens, cols = a_ref.shape
    projected = a_ref[0].astype(f32)
    for piece in range(1, count):
        projected = projected + a_ref[piece].astype(f32)
    columns = lax.broadcasted_iota(jnp.int32, (tokens, cols), 1) + pl.program_id(0) * cols
    target = jnp.where(l_ref[...] == columns, 1.0, 0.0)
    residual = ((projected - target) / total_tokens).astype(bf16)
    for piece in range(count):
        o_ref[piece] = residual


def spread_residual(arrived, labels, total_tokens):
    count, tokens, width = arrived.shape
    spec = pl.BlockSpec((count, tokens, width // 2), lambda i: (0, 0, i))
    return pl.pallas_call(
        functools.partial(residual_kernel, total_tokens),
        grid=(2,),
        in_specs=[spec, pl.BlockSpec((tokens, 1), lambda i: (0, 0))],
        out_specs=spec,
        out_shape=pltpu.HBM(arrived.shape, bf16),
        compiler_params=params(),
        cost_estimate=cost(0, 4 * arrived.size),
    )(arrived, labels)


def average_kernel(scale, a_ref, o_ref):
    total = a_ref[0].astype(f32)
    for piece in range(1, a_ref.shape[0]):
        total = total + a_ref[piece].astype(f32)
    averaged = (total / scale).astype(bf16)
    for piece in range(a_ref.shape[0]):
        o_ref[piece] = averaged


def spread_average(arrived, scale):
    return pl.pallas_call(
        functools.partial(average_kernel, scale),
        out_shape=jax.ShapeDtypeStruct(arrived.shape, bf16),
        compiler_params=params(),
        cost_estimate=cost(0, 4 * arrived.size),
    )(arrived)


def adam(count, grad, weights, moment_one, moment_two):
    moment_one = beta_one * moment_one + (1.0 - beta_one) * grad
    moment_two = beta_two * moment_two + ((1.0 - beta_two) * grad) * grad
    corrected = moment_two * (1.0 / (1.0 - beta_two**count))
    root = corrected * lax.rsqrt(corrected)
    scaled = (inner_rate / (1.0 - beta_one**count)) * moment_one
    weights = (1.0 - inner_rate * decay_rate) * weights - scaled * pltpu.reciprocal(root + adam_eps)
    return weights, moment_one, moment_two


def turned_dot(x, r):
    return lax.dot_general(x, r, (((0,), (0,)), ((), ())), preferred_element_type=f32)


def middle_kernel(x_ref, r_ref, w_ref, m_ref, v_ref, wo_ref, mo_ref, vo_ref, rounded_ref):
    weights, moment_one, moment_two = adam(
        1,
        turned_dot(flat(x_ref), flat(r_ref)),
        w_ref[...].astype(f32),
        m_ref[0].astype(f32),
        v_ref[0].astype(f32),
    )
    wo_ref[...] = weights
    mo_ref[...] = moment_one
    vo_ref[...] = moment_two
    rounded_ref[...] = weights.astype(bf16)


def middle(features, residual, weights, first, second):
    pieces, tokens, rows = features.shape
    width = weights.shape[1]
    block = BLOCK
    state = jax.ShapeDtypeStruct((rows, width), f32)
    state_spec = pl.BlockSpec((block, width), lambda i: (i, 0))
    moment_spec = pl.BlockSpec((1, block, width), lambda i: (0, i, 0))
    return pl.pallas_call(
        middle_kernel,
        grid=(rows // block,),
        in_specs=[
            pl.BlockSpec((pieces, tokens, block), lambda i: (0, 0, i)),
            pl.BlockSpec((pieces, tokens, width), lambda i: (0, 0, 0)),
            state_spec,
            moment_spec,
            moment_spec,
        ],
        out_specs=[state_spec] * 4,
        out_shape=[state] * 3 + [jax.ShapeDtypeStruct((rows, width), bf16)],
        compiler_params=params(),
        cost_estimate=cost(2 * pieces * tokens * rows * width, 26 * rows * width),
    )(features, residual, weights, first, second)


def last_kernel(place_ref, x_ref, r_ref, g_ref, w_ref, m_ref, v_ref, mine_ref, other_ref):
    grad = turned_dot(flat(x_ref), flat(r_ref))
    weights, _, _ = adam(INNER, grad, w_ref[...], m_ref[...], v_ref[...])
    change = g_ref[...].astype(f32) - weights
    step, half = pl.program_id(0), pl.num_programs(0) // 2

    @pl.when(step < half)
    def _():
        other_ref[...] = change.astype(bf16)

    @pl.when(step >= half)
    def _():
        mine_ref[...] = change


def last(place, features, residual, start, state):
    pieces, tokens, rows = features.shape
    width = start.shape[1]
    block = BLOCK
    steps = rows // block
    half = steps // 2

    def row(i, p):
        return lax.rem(i + half * (1 + p[0]), steps)

    state_spec = pl.BlockSpec((block, width), lambda i, p: (row(i, p), 0))
    return pl.pallas_call(
        last_kernel,
        grid_spec=pltpu.PrefetchScalarGridSpec(
            num_scalar_prefetch=1,
            grid=(steps,),
            in_specs=[
                pl.BlockSpec((pieces, tokens, block), lambda i, p: (0, 0, row(i, p))),
                pl.BlockSpec((pieces, tokens, width), lambda i, p: (0, 0, 0)),
            ]
            + [state_spec] * 4,
            out_specs=[
                pl.BlockSpec((block, width), lambda i, p: (jnp.maximum(i - half, 0), 0)),
                pl.BlockSpec((block, width), lambda i, p: (jnp.minimum(i, half - 1), 0)),
            ],
        ),
        out_shape=[
            jax.ShapeDtypeStruct((rows // 2, width), f32),
            jax.ShapeDtypeStruct((rows // 2, width), bf16),
        ],
        compiler_params=params(),
        cost_estimate=cost(2 * pieces * tokens * rows * width, 20 * rows * width),
    )(place, features, residual, start, *state)


def outer_kernel(
    place_ref, near_left, far_left, near_low, near_high, far_low, far_high, near_mom, far_mom,
    mine_ref, other_ref, g_ref, own_ref, new_ref, new_mom_ref, left, kept,
):
    side, row = pl.program_id(0), pl.program_id(1)
    half, width = mine_ref.shape

    def square(ref):
        return ref[...].reshape(half, half)

    @pl.when(side == 0)
    def _():
        left_part = jnp.dot(square(near_left), mine_ref[...], preferred_element_type=f32) + jnp.dot(
            square(far_left), other_ref[...], preferred_element_type=f32
        )
        left[row] = left_part.astype(bf16)

    def finish(first, second, mom_ref):
        precond = jnp.dot(left[row, :, :half], square(first), preferred_element_type=f32) + jnp.dot(
            left[row, :, half:], square(second), preferred_element_type=f32
        )
        momentum = outer_mom * square(mom_ref).astype(f32) + precond
        new_ref[...] = (
            g_ref[...].astype(f32) - outer_rate * (precond + outer_mom * momentum)
        ).astype(bf16)
        owned = own_ref.shape[0]
        per = half // owned

        @pl.when(row == place_ref[1] // per)
        def _():
            kept[...] = precond
            start = pl.multiple_of(lax.rem(place_ref[1], per) * owned, owned)
            new_mom_ref[...] = outer_mom * own_ref[...] + kept[pl.ds(start, owned), :]

    @pl.when(side == 0)
    def _():
        finish(near_low, near_high, near_mom)

    @pl.when(side == 1)
    def _():
        finish(far_low, far_high, far_mom)


def outer(place, near, far, mine, other, start, momentum):
    depth, _, cores, _, owned, half = near.shape
    width = mine.shape[1]
    near, far = apart(near), apart(far)

    def piece(what, row):
        return pl.BlockSpec(
            (depth, 1, cores, 1, owned, half), lambda j, i, p: (0, row(i), 0, what, 0, 0)
        )

    def here(i):
        return i

    def column(j, p):
        return lax.rem(p[0] + j, 2)

    low, high = (lambda i: 0), (lambda i: 1)
    whole = pl.BlockSpec((half, width), lambda j, i, p: (0, 0))
    own_spec = pl.BlockSpec((owned, half), lambda j, i, p: (0, column(j, p)))
    new_spec = pl.BlockSpec((half, half), lambda j, i, p: (i, column(j, p)))
    return pl.pallas_call(
        outer_kernel,
        grid_spec=pltpu.PrefetchScalarGridSpec(
            num_scalar_prefetch=1,
            grid=(2, 2),
            in_specs=[
                piece(0, here),
                piece(0, here),
                piece(1, low),
                piece(1, high),
                piece(1, low),
                piece(1, high),
                piece(2, here),
                piece(2, here),
                whole,
                whole,
                new_spec,
                own_spec,
            ],
            out_specs=[new_spec, own_spec],
            scratch_shapes=[
                pltpu.VMEM((2, half, width), bf16),
                pltpu.VMEM((half, half), f32),
            ],
        ),
        out_shape=[
            jax.ShapeDtypeStruct((2 * half, width), bf16),
            jax.ShapeDtypeStruct((owned, width), f32),
        ],
        compiler_params=params(),
        cost_estimate=cost(4 * width**3, 14 * width * width),
    )(place, near, far, near, near, far, far, near, far, mine, other, apart(start), momentum)


def shards(
    global_params, first_moment, second_moment, batch, labels, momentum, left_root, right_root
):
    rows, width = global_params.shape
    tokens = batch.shape[2]
    fsdp = lax.axis_size("fsdp")
    replicas = lax.axis_size("rep")
    owned = rows // replicas
    total_tokens = tokens * fsdp
    half = rows // 2
    own_index = lax.axis_index("rep")
    core = own_index % 2
    upper = own_index // (replicas // 2)

    def stamp(kind):
        return jnp.stack([core, own_index, own_index * 4 + kind]).astype(jnp.int32)

    chips = replicas // 2
    depth = chips // 2
    swap = [(i, i ^ 1) for i in range(replicas)]
    beside = [(i, i ^ chips) for i in range(replicas)]
    same_core = [[2 * k + c for k in range(chips)] for c in range(2)]
    column = [[x * chips + 2 * z + c for z in range(depth)] for x in range(2) for c in range(2)]
    targets = [labels[0, step].reshape(tokens, 1) for step in range(INNER)]

    features = exchange(split_batch(batch, 0, fsdp), "fsdp")
    split = split_batch(batch, 1, fsdp)
    partial = partial_of(features, global_params, split)

    def ordered(index, own, partner):
        return jnp.where(index == 0, jnp.stack([own, partner]), jnp.stack([partner, own]))

    def own_residual(partial, step):
        return spread_residual(exchange(partial, "fsdp"), targets[step], total_tokens)

    own = own_residual(partial, 0)
    residual = exchange(own, "fsdp")
    kept, sent = pack(stamp(1), left_root, right_root, momentum, own)
    two = ordered(core, kept, lax.ppermute(sent, "rep", swap))
    four = ordered(upper, two, lax.ppermute(two, "rep", beside))
    near = lax.all_gather(four, "rep", axis=0, axis_index_groups=column)
    far = lax.ppermute(near, "rep", swap)
    following = exchange(hold(split, residual, four), "fsdp")
    *state, rounded = middle(
        features, residual, global_params, apart(first_moment), apart(second_moment)
    )
    state = [apart(x) for x in state]
    partial = partial_of(following, apart(rounded), residual)
    mine, sent = last(stamp(3), following, exchange(own_residual(partial, 1), "fsdp"), global_params, state)
    pair = (mine + lax.ppermute(sent, "rep", swap).astype(f32)).astype(bf16)
    arrived = exchange(pair.reshape(chips, owned, width), "rep", same_core)
    averaged = exchange(spread_average(arrived, replicas), "rep", same_core).reshape(half, width)
    other = lax.ppermute(averaged, "rep", swap)
    return tuple(outer(stamp(5), near, far, averaged, other, global_params, momentum))


def solution(mesh):
    in_specs = (
        P("fsdp", None),
        P("rep", "fsdp", None),
        P("rep", "fsdp", None),
        P("rep", None, "fsdp", None),
        P("rep", None, "fsdp"),
        P(("fsdp", "rep"), None),
        P(("fsdp", "rep"), None),
        P("fsdp", "rep", None),
    )
    out_specs = (P("fsdp", None), P(("fsdp", "rep"), None))
    return jax.shard_map(shards, mesh=mesh, in_specs=in_specs, out_specs=out_specs, check_vma=False)
```
